512 devices in a mesh: replica: 4 (over x), vocab: 16 (over z_lo, core), dp: 8 (over z_hi, y).
Axes of the slice: x: 4, y: 4, z: 16 (z_hi: 2, z_lo: 8; z = z_hi * 8 + z_lo), core: 2. Of those that a mesh axis runs over, the one named last changes fastest.
Arguments:
- hidden: bfloat16 [4, 512, 1792], P('replica', 'dp'), may hold values from -16 to 16
- head_weight: bfloat16 [4, 1792, 131072], P('replica', None, ('vocab', 'dp')), may hold values from -1 to 1
- targets: int32 [512], P('dp'), may hold values from 0 to 131071
- pairing: int32 [4], replicated, may hold values from 0 to 3, as said below
- token_weight: float32 [4, 512], P('replica', 'dp'), may hold values from 1 to 10
Outputs:
- grad_hidden: bfloat16 [4, 512, 1792], P('replica', 'dp')
- token_loss: float32 [4, 512], P('replica', 'dp')
The draws below stay inside these ranges and needn't reach their ends.
Inputs may be any that keep to these rules, and one draw needn't show every extreme that they name: pairing[r] is the replica whose predictions replica r learns from; following pairing from any replica visits all four replicas once before returning, and one of its steps goes to the replica two indices away.
All inputs are finite; a program needn't handle non-finite values.
Results may differ from the reference program's by a relative error of at most 0.015.
Values may be sent and summed in bfloat16 or wider, within the bound.
No kernel may reach another device: no remote copies, remote signals or barrier semaphores. Data moves between devices by JAX's collectives and lax.ppermute only.
A program may use at most 64 MiB of HBM per device.

```python
import math
import jax
import jax.numpy as jnp
import numpy as np
from jax import lax

D = 1792
TOKENS = 512
VOCAB = 131072
REPLICAS = 4


def head_column(key, column):
    return jax.random.normal(jax.random.fold_in(key, column), (REPLICAS, D), jnp.float32) * (3.0 / math.sqrt(D))


def draw_head_weight(key, part):
    columns = jax.vmap(lambda column: head_column(key, column))(jnp.arange(VOCAB, dtype=jnp.int32))
    return jnp.clip(jnp.transpose(columns, (1, 2, 0)), -1.0, 1.0).astype(jnp.bfloat16)


def draw_hidden(key, part):
    key = jax.random.fold_in(key, 5)
    values = jax.random.normal(key, (REPLICAS, TOKENS, D), jnp.float32)
    return jnp.clip(values, -6.0, 6.0).astype(jnp.bfloat16)


def draw_pairing(key, part):
    key = jax.random.fold_in(key, 3)
    start = jax.random.randint(jax.random.fold_in(key, 1), (), 0, 4).astype(jnp.int32)
    flip = jax.random.randint(jax.random.fold_in(key, 2), (), 0, 2).astype(jnp.int32)
    order = jnp.stack([start, (start + 2) % 4, (start + 1 + 2 * flip) % 4, (start + 3 - 2 * flip) % 4]).astype(jnp.int32)
    following = jnp.roll(order, -1)
    return jnp.zeros((REPLICAS,), jnp.int32).at[order].set(following)


def set_ends(drawn, own_key, least, top_value):
    extent = drawn.shape
    index_at = [jax.random.randint(jax.random.fold_in(own_key, axis), (), 0, extent[axis]) for axis in range(len(extent))]
    drawn = drawn.at[tuple(index_at)].set(least)
    longest = extent.index(max(extent))
    index_at[longest] = (index_at[longest] + 1) % extent[longest]
    return drawn.at[tuple(index_at)].set(top_value)


def levels(stream_key, shape, pieces, least, largest):
    def one(axis_at, shards_of):
        steps = jax.random.uniform(jax.random.fold_in(jax.random.fold_in(stream_key, 6), axis_at), (shards_of,), jnp.float32, least / len(pieces), largest / len(pieces))
        return jnp.repeat(jnp.exp(steps), shape[axis_at] // shards_of).reshape((-1,) + (1,) * (len(shape) - axis_at - 1))

    gain = one(*pieces[0])
    for cut in pieces[1:]:
        gain = gain * one(*cut)
    return gain


def ranked_wide(rng, dims, amount, slope):
    weights = [min(1 << octave, amount + 1 - (1 << octave)) * (1 << 20) // math.isqrt((1 << octave) ** slope) + 1 for octave in range((amount + 1).bit_length()) if 1 << octave <= amount]
    width = 1 + sum(weights) // (1 << 30)
    grid = np.cumsum(np.array([max(1, weight // width) for weight in weights]))
    lot = jax.random.randint(jax.random.fold_in(rng, 1), dims, 0, int(grid[len(weights) - 1]))
    start = jnp.left_shift(1, jnp.searchsorted(jnp.asarray(grid, jnp.int32), lot, side="right").astype(jnp.int32))
    standing = start - 1 + jax.random.randint(jax.random.fold_in(rng, 4), dims, 0, 1 << 30) % jnp.minimum(start, amount + 1 - start)
    return jax.random.permutation(jax.random.fold_in(rng, 2), amount)[standing].astype(jnp.int32)


def setup_inputs(seed: int = 0) -> dict:
    streams_of = jax.random.split(jax.random.key(seed), 6)
    return {
        "hidden": draw_hidden(jax.random.fold_in(streams_of[5], 71), 0),
        "head_weight": draw_head_weight(jax.random.fold_in(streams_of[5], 71), 0),
        "targets": set_ends(ranked_wide(streams_of[2], (TOKENS,), VOCAB, 2), jax.random.fold_in(streams_of[2], 3), 0, VOCAB - 1).astype(jnp.int32),
        "pairing": draw_pairing(jax.random.fold_in(streams_of[5], 71), 0),
        "token_weight": jnp.clip(jnp.exp(math.log(10.0) - 2.3025851 * jax.random.uniform(streams_of[4], (REPLICAS, TOKENS), jnp.float32) ** levels(streams_of[4], (REPLICAS, TOKENS), ((0, 4), (1, 8)), -0.2, 0.2)), 1.0, 10.0),
    }


kl_weight = 1.0


def log_probs(hidden_rows, head_rows):
    logits = jnp.dot(hidden_rows, head_rows, preferred_element_type=jnp.float32)
    row_top = jnp.max(logits, axis=1)
    log_total = row_top + jnp.log(jnp.sum(jnp.exp(logits - row_top[:, None]), axis=1))
    return logits, log_total


def reference(hidden, head_weight, targets, pairing, token_weight):
    def first_pass(inputs):
        logits, log_total = log_probs(inputs[0], inputs[1])
        return logits - log_total[:, None]

    sources = lax.map(first_pass, (hidden, head_weight))
    columns = jnp.arange(VOCAB, dtype=jnp.int32)
    onehot = (columns[None, :] == targets[:, None]).astype(jnp.float32)

    def second_pass(inputs):
        hidden_rows, head_rows, weights, replica = inputs
        logits, log_total = log_probs(hidden_rows, head_rows)
        own_logp = logits - log_total[:, None]
        own_prob = jnp.exp(own_logp)
        partner = pairing[replica]
        peer_logp = lax.dynamic_index_in_dim(sources, partner, 0, keepdims=False)
        peer_prob = jnp.exp(peer_logp)
        log_ratio = own_logp - peer_logp
        kl_forward = jnp.sum(peer_prob * (-log_ratio), axis=1)
        kl_reverse = jnp.sum(own_prob * log_ratio, axis=1)
        target_logit = jnp.take_along_axis(logits, targets[:, None], axis=1)[:, 0]
        losses = weights * (log_total - target_logit + 0.5 * kl_weight * (kl_forward + kl_reverse))
        inner = own_prob - onehot + 0.5 * kl_weight * ((own_prob - peer_prob) + own_prob * (log_ratio - kl_reverse[:, None]))
        logit_grad = (weights[:, None] * inner).astype(jnp.bfloat16)
        grads = lax.dot_general(logit_grad, head_rows, (((1,), (1,)), ((), ())), preferred_element_type=jnp.float32)
        return grads.astype(jnp.bfloat16), losses

    grad_hidden, token_loss = lax.map(second_pass, (hidden, head_weight, token_weight, jnp.arange(REPLICAS, dtype=jnp.int32)))
    return grad_hidden, token_loss
```

```python
import functools

import jax
import jax.numpy as jnp
from jax import lax
from jax.experimental import pallas as pl
from jax.experimental.pallas import tpu as pltpu
from jax.sharding import Mesh
from jax.sharding import PartitionSpec as P

kl_weight = 1.0
F32 = jnp.float32
BF16 = jnp.bfloat16
R = 4
Z = ("zh", "zl")
FAR = {0: 12, 1: 13, 2: 14, 3: 15, 4: 8, 5: 9, 6: 10, 7: 11}
FAR.update({b: a for a, b in FAR.items()})
SWAP_Z = [(z % 8 * 2 + z // 8, FAR[z] % 8 * 2 + FAR[z] // 8) for z in range(16)]
SWAP_C = [(0, 1), (1, 0)]


def forward_kernel(half_ref, mine_ref, other_ref, w_mine_ref, w_other_ref, out_ref):
    depth = w_mine_ref.shape[1]
    out_ref[...] = jnp.dot(
        mine_ref[:, :depth], w_mine_ref[0], preferred_element_type=F32
    ) + jnp.dot(other_ref[:, :depth], w_other_ref[0], preferred_element_type=F32)


def forward(half, mine, other, head):
    rows, depth, cols = mine.shape[0], head.shape[1] // 2, head.shape[2]
    tile = 256
    return pl.pallas_call(
        forward_kernel,
        out_shape=jax.ShapeDtypeStruct((rows, cols), F32),
        grid_spec=pltpu.PrefetchScalarGridSpec(
            num_scalar_prefetch=1,
            grid=(cols // tile,),
            in_specs=[
                pl.BlockSpec(mine.shape, lambda n, h: (0, 0)),
                pl.BlockSpec(other.shape, lambda n, h: (0, 0)),
                pl.BlockSpec((1, depth, tile), lambda n, h: (0, h[0], n)),
                pl.BlockSpec((1, depth, tile), lambda n, h: (0, 1 - h[0], n)),
            ],
            out_specs=pl.BlockSpec((rows, tile), lambda n, h: (0, n)),
        ),
        compiler_params=pltpu.CompilerParams(vmem_limit_bytes=40 << 20),
        name="logits",
    )(half, mine, other, head, head)


def stats_kernel(pair_ref, tgt_ref, l_ref, out_ref, cols_ref):
    step = pl.program_id(0)
    rows, vocab = l_ref.shape[1], l_ref.shape[2]
    lane = lax.broadcasted_iota(jnp.int32, (rows, 128), 1)
    hit = lax.broadcasted_iota(jnp.int32, (rows, vocab), 1) == tgt_ref[...]
    for r in range(R):
        learner = jnp.int32(0)
        for k in range(R):
            learner = jnp.where(pair_ref[k] == r, k, learner)
        logits = l_ref[r]
        top = jnp.max(logits, axis=1, keepdims=True)
        power = jnp.exp(logits - top)
        total = jnp.sum(power, axis=1, keepdims=True)
        to_peer = jnp.sum(power * (logits - l_ref[pair_ref[r]]), axis=1, keepdims=True)
        to_learner = jnp.sum(power * (logits - l_ref[learner]), axis=1, keepdims=True)
        target = jnp.sum(jnp.where(hit, logits, 0.0), axis=1, keepdims=True)
        packed = jnp.zeros((rows, 128), F32)
        for i, v in enumerate((top, total, to_peer, to_learner, target)):
            packed = jnp.where(lane == i, v, packed)
        cols_ref[r, pl.ds(pl.multiple_of(step * rows, rows), rows), :] = packed

    @pl.when(step == pl.num_programs(0) - 1)
    def _():
        for r in range(R):
            flat = jnp.transpose(cols_ref[r])[:8]
            for k in range(out_ref.shape[0]):
                out_ref[k, r] = flat


def stats(pairing, tgt, logits, copies):
    rows, vocab = logits.shape[1], logits.shape[2]
    tile = 32
    return pl.pallas_call(
        stats_kernel,
        out_shape=jax.ShapeDtypeStruct((copies, R, 8, rows), F32),
        grid_spec=pltpu.PrefetchScalarGridSpec(
            num_scalar_prefetch=1,
            grid=(rows // tile,),
            in_specs=[
                pl.BlockSpec((tile, 1), lambda n, p: (n, 0)),
                pl.BlockSpec((R, tile, vocab), lambda n, p: (0, n, 0)),
            ],
            out_specs=pl.BlockSpec((copies, R, 8, rows), lambda n, p: (0, 0, 0, 0)),
            scratch_shapes=[pltpu.VMEM((R, rows, 128), F32)],
        ),
        compiler_params=pltpu.CompilerParams(vmem_limit_bytes=24 << 20),
        name="local_stats",
    )(pairing, tgt, logits)


def merged(parts):
    top = jnp.max(parts[:, :, 0], axis=0)
    scale = jnp.exp(parts[:, :, 0] - top[None])
    sums = [jnp.sum(parts[:, :, i] * scale, axis=0) for i in (1, 2, 3)]
    return [top] + sums + [jnp.sum(parts[:, :, 4], axis=0)]


def merge_kernel(in_ref, out_ref):
    values = merged(in_ref[...])
    for k in range(out_ref.shape[0]):
        for i, v in enumerate(values):
            out_ref[k, :, i, :] = v
        for i in range(len(values), 8):
            out_ref[k, :, i, :] = jnp.zeros_like(values[0])


def merge(parts, copies):
    return pl.pallas_call(
        merge_kernel,
        out_shape=jax.ShapeDtypeStruct((copies,) + parts.shape[1:], F32),
        compiler_params=pltpu.CompilerParams(vmem_limit_bytes=24 << 20),
        name="merge_stats",
    )(parts)


def grad_kernel(pair_ref, parts_ref, tgt_ref, l_ref, out_ref, flat_ref, cols_ref, prob_ref):
    step = pl.program_id(0)
    last = pl.num_programs(0) - 1
    rows, vocab = l_ref.shape[1], l_ref.shape[2]

    @pl.when(step == 0)
    def _():
        top, total, to_peer, to_learner, target = merged(parts_ref[...])
        log_total = top + jnp.log(total)
        flat_ref[...] = jnp.zeros_like(flat_ref)
        flat_ref[:, 0, :] = log_total
        flat_ref[:, 4, :] = to_peer / total
        flat_ref[:, 5, :] = to_learner / total
        flat_ref[:, 6, :] = target
        for r in range(R):
            peer = pair_ref[r]
            own_total, peer_total = flat_ref[r, 0:1, :], flat_ref[peer, 0:1, :]
            reverse = flat_ref[r, 4:5, :] - (own_total - peer_total)
            forward_kl = flat_ref[peer, 5:6, :] - (peer_total - own_total)
            flat_ref[r, 1:2, :] = peer_total
            flat_ref[r, 2:3, :] = reverse
            flat_ref[r, 3:4, :] = (
                own_total - flat_ref[r, 6:7, :] + 0.5 * kl_weight * (forward_kl + reverse)
            )
        for r in range(R):
            cols_ref[r] = jnp.transpose(flat_ref[r])

    @pl.when(step < last)
    def _():
        at = pl.ds(pl.multiple_of(step * rows, rows), rows)
        hit = lax.broadcasted_iota(jnp.int32, (rows, vocab), 1) == tgt_ref[...]
        onehot = jnp.where(hit, 1.0, 0.0)
        for r in range(R):
            prob_ref[r] = jnp.exp(l_ref[r] - cols_ref[r, at, 0:1])
        for r in range(R):
            peer = pair_ref[r]
            own_prob = prob_ref[r]
            ratio = (l_ref[r] - cols_ref[r, at, 0:1]) - (l_ref[peer] - cols_ref[r, at, 1:2])
            inner = (
                own_prob
                - onehot
                + 0.5
                * kl_weight
                * ((own_prob - prob_ref[peer]) + own_prob * (ratio - cols_ref[r, at, 2:3]))
            )
            out_ref[r] = inner.astype(BF16)

    @pl.when(step == last)
    def _():
        out_ref[...] = jnp.zeros_like(out_ref)
        row = lax.broadcasted_iota(jnp.int32, (out_ref.shape[1], 128), 0)
        for r in range(R):
            loss = flat_ref[r, 3:4, :]
            high = loss.astype(BF16).astype(F32)
            middle = (loss - high).astype(BF16).astype(F32)
            low = (loss - high) - middle
            pieces = jnp.where(
                row == 0, high, jnp.where(row == 1, middle, jnp.where(row == 2, low, 0.0))
            )
            out_ref[r, :, 0:128] = pieces.astype(BF16)


def logit_grads(pairing, parts, tgt, logits):
    rows, vocab = logits.shape[1], logits.shape[2]
    tile = 16
    steps = rows // tile
    return pl.pallas_call(
        grad_kernel,
        out_shape=jax.ShapeDtypeStruct((R, rows + tile, vocab), BF16),
        grid_spec=pltpu.PrefetchScalarGridSpec(
            num_scalar_prefetch=1,
            grid=(steps + 1,),
            in_specs=[
                pl.BlockSpec(parts.shape, lambda n, p: (0, 0, 0, 0)),
                pl.BlockSpec((tile, 1), lambda n, p: (jnp.minimum(n, steps - 1), 0)),
                pl.BlockSpec((R, tile, vocab), lambda n, p: (0, jnp.minimum(n, steps - 1), 0)),
            ],
            out_specs=pl.BlockSpec((R, tile, vocab), lambda n, p: (0, n, 0)),
            scratch_shapes=[
                pltpu.VMEM((R, 128, 128), F32),
                pltpu.VMEM((R, 128, 128), F32),
                pltpu.VMEM((R, tile, vocab), F32),
            ],
        ),
        compiler_params=pltpu.CompilerParams(vmem_limit_bytes=24 << 20),
        name="logit_grads",
    )(pairing, parts, tgt, logits)


def backward_kernel(half_ref, g_ref, w_ref, out_ref):
    part = g_ref.shape[1] - 16
    g = g_ref[:, :part, :].reshape(R * part, g_ref.shape[2])
    out_ref[...] = lax.dot_general(
        g, w_ref[0], (((1,), (1,)), ((), ())), preferred_element_type=F32
    ).astype(out_ref.dtype)


def backward(half, grads, head, dtype):
    rows, depth, cols = R * (grads.shape[1] - 16), head.shape[1] // 2, head.shape[2]
    tile = 128
    tiles = depth // tile
    return pl.pallas_call(
        backward_kernel,
        out_shape=jax.ShapeDtypeStruct((rows, depth), dtype),
        grid_spec=pltpu.PrefetchScalarGridSpec(
            num_scalar_prefetch=1,
            grid=(tiles,),
            in_specs=[
                pl.BlockSpec(grads.shape, lambda n, h: (0, 0, 0)),
                pl.BlockSpec((1, tile, cols), lambda n, h: (0, h[0] * tiles + n, 0)),
            ],
            out_specs=pl.BlockSpec((rows, tile), lambda n, h: (0, n)),
        ),
        compiler_params=pltpu.CompilerParams(vmem_limit_bytes=40 << 20),
        name="head_grads",
    )(half, grads, head)


def on_device(hidden, head_weight, targets, pairing, token_weight):
    x, zl, c, zh, y = (lax.axis_index(a) for a in ("x", "zl", "c", "zh", "y"))
    rows, features = hidden.shape[1], hidden.shape[2]
    depth = features // 2
    vocab = head_weight.shape[2]
    offset = (((zl * 2 + c) * 2 + zh) * 4 + y) * vocab
    half = c.reshape(1)

    ids = jnp.stack([targets >> 12, (targets >> 6) & 63, targets & 63], axis=1).astype(BF16)
    mine = jnp.concatenate(
        [
            lax.dynamic_slice_in_dim(hidden[0], c * depth, depth, 1),
            jnp.pad(ids, ((0, 0), (0, 125))),
        ],
        axis=1,
    )
    far = lax.ppermute(mine, ("zl", "zh"), SWAP_Z)
    both = jnp.where(zh == 0, jnp.stack([mine, far]), jnp.stack([far, mine]))
    both = both.reshape(2 * rows, depth + 128)
    all_mine = lax.all_to_all(jnp.broadcast_to(both[None], (4,) + both.shape), "y", 0, 0)
    all_mine = all_mine.reshape(8 * rows, depth + 128)
    all_other = lax.ppermute(all_mine, "c", SWAP_C)

    logits = forward(half, all_mine, all_other, head_weight).reshape(R, 2 * rows, vocab)
    sources = lax.all_to_all(logits, "x", 0, 0)
    ids = lax.dynamic_slice(all_mine, (x * 2 * rows, depth), (2 * rows, 3)).astype(jnp.int32)
    tgt = ((ids[:, 0:1] << 12) | (ids[:, 1:2] << 6) | ids[:, 2:3]) - offset

    local = stats(pairing, tgt, sources, 8)
    near = merge(lax.all_to_all(local, ("c", "y"), 0, 0), 16)
    parts = lax.all_to_all(near, Z, 0, 0)
    grads = lax.all_to_all(logit_grads(pairing, parts, tgt, sources), "x", 0, 0)

    loss = lax.dynamic_slice(grads, (y, 2 * rows, zh * rows), (1, 3, rows))[0].astype(F32)
    losses = token_weight[0] * (loss[0] + (loss[1] + loss[2]))

    sent = lax.ppermute(backward(1 - half, grads, head_weight, BF16), "c", SWAP_C)
    kept = backward(half, grads, head_weight, F32)
    by_y = (kept + sent.astype(F32)).astype(BF16).reshape(4, 2 * rows, depth)
    by_y = lax.all_to_all(by_y, "y", 0, 0)
    by_z = jnp.sum(by_y.astype(F32), axis=0).astype(BF16).reshape(16, rows // 8, depth)
    by_z = lax.all_to_all(by_z, Z, 0, 0)
    weights = lax.dynamic_slice_in_dim(token_weight[0], zl * (rows // 8), rows // 8, 0)
    final = (jnp.sum(by_z.astype(F32), axis=0) * weights[:, None]).astype(BF16)
    final = lax.all_to_all(
        jnp.broadcast_to(final[None], (16,) + final.shape), ("zl", "c"), 0, 0
    )
    final = final.reshape(8, 2, rows // 8, depth).transpose(0, 2, 1, 3).reshape(rows, features)
    return (final[None], losses[None])


def solution(mesh):
    fine = Mesh(mesh.devices.reshape(4, 8, 2, 2, 4), ("x", "zl", "c", "zh", "y"))
    return jax.shard_map(
        on_device,
        mesh=fine,
        in_specs=(
            P("x", ("zh", "y"), None),
            P("x", None, ("zl", "c", "zh", "y")),
            P(("zh", "y")),
            P(),
            P("x", ("zh", "y")),
        ),
        out_specs=(P("x", ("zh", "y"), None), P("x", ("zh", "y"))),
        check_vma=False,
    )
```

```python
import functools

import jax
import jax.numpy as jnp
from jax import lax
from jax.experimental import pallas as pl
from jax.experimental.pallas import tpu as pltpu
from jax.sharding import Mesh
from jax.sharding import PartitionSpec as P

kl_weight = 1.0
F32 = jnp.float32
BF16 = jnp.bfloat16
Z = ("zh", "zl")
FAR = {0: 12, 1: 13, 2: 14, 3: 15, 4: 8, 5: 9, 6: 10, 7: 11}
FAR.update({b: a for a, b in FAR.items()})
SWAP_Z = [(z % 8 * 2 + z // 8, FAR[z] % 8 * 2 + FAR[z] // 8) for z in range(16)]
SWAP_C = [(0, 1), (1, 0)]
PAIRINGS = ((2, 3, 1, 0), (3, 2, 0, 1), (1, 3, 0, 2), (2, 0, 3, 1))
LANES = 128
TILE = 32


def call(kernel, outs, operands, name, scratch=(), flops=0):
    scalars = [o.ndim == 1 for o in operands]
    vmem, smem = pl.BlockSpec(memory_space=pltpu.VMEM), pl.BlockSpec(memory_space=pltpu.SMEM)
    moved = sum(o.size * o.dtype.itemsize for o in list(operands) + list(outs))
    return pl.pallas_call(
        kernel,
        out_shape=outs if len(outs) > 1 else outs[0],
        in_specs=[smem if s else vmem for s in scalars],
        out_specs=[vmem] * len(outs) if len(outs) > 1 else vmem,
        scratch_shapes=scratch,
        compiler_params=pltpu.CompilerParams(vmem_limit_bytes=moved + (6 << 20)),
        cost_estimate=pl.CostEstimate(flops=flops, bytes_accessed=moved, transcendentals=0),
        name=name,
    )(*operands)


def shape(*dims, dtype=F32):
    return jax.ShapeDtypeStruct(dims, dtype)


def tiles(rows, step=TILE):
    def run(body):
        def at(i, carry):
            body(pl.ds(pl.multiple_of(i * step, step), step))
            return carry

        lax.fori_loop(0, rows // step, at, 0)

    return run


def packed(values, rows):
    lane = lax.broadcasted_iota(jnp.int32, (rows, LANES), 1)
    out = jnp.zeros((rows, LANES), F32)
    for i, v in enumerate(values):
        if v is not None:
            out = jnp.where(lane == i, v, out)
    return out


def forward_kernel(h_ref, w_ref, x_ref, sent_ref, top_ref):
    width = w_ref.shape[2]
    at = pl.ds(pl.multiple_of(pl.program_id(0) * width, width), width)
    x_ref[:, at] = jnp.dot(h_ref[...], w_ref[0], preferred_element_type=F32)

    @pl.when(pl.program_id(0) == pl.num_programs(0) - 1)
    def _():
        below_top(x_ref, sent_ref, top_ref)


def below_top(x_ref, sent_ref, top_ref):
    rows, vocab = x_ref.shape

    @tiles(rows)
    def _(at):
        logits = x_ref[at]
        top = jnp.max(logits, axis=1, keepdims=True)
        below = logits - top
        x_ref[at] = below
        square = below * below
        sent_ref[at] = (square * square).astype(BF16)
        top_ref[at] = jnp.broadcast_to(top, (TILE, LANES))

    row = lax.broadcasted_iota(jnp.int32, (16, LANES), 0)
    sent_ref[rows:] = jnp.zeros((16, vocab), BF16)
    for b in range(rows // LANES):
        top = jnp.transpose(top_ref[b * LANES : (b + 1) * LANES])[:16]
        high = top.astype(BF16).astype(F32)
        middle = (top - high).astype(BF16).astype(F32)
        low = (top - high) - middle
        pieces = jnp.where(row == 0, high, jnp.where(row == 1, middle, low))
        pieces = jnp.where(row < 3, pieces, 0.0)
        sent_ref[rows:, b * LANES : (b + 1) * LANES] = pieces.astype(BF16)


def forward(h, head):
    rows, features, vocab = h.shape[0], h.shape[1], head.shape[2]
    width = 256
    outs = [shape(rows, vocab), shape(rows + 16, vocab, dtype=BF16), shape(rows, LANES)]
    return pl.pallas_call(
        forward_kernel,
        out_shape=outs,
        grid=(vocab // width,),
        in_specs=[
            pl.BlockSpec(h.shape, lambda n: (0, 0)),
            pl.BlockSpec((1, features, width), lambda n: (0, 0, n)),
        ],
        out_specs=[pl.BlockSpec(o.shape, lambda n: (0, 0)) for o in outs],
        compiler_params=pltpu.CompilerParams(vmem_limit_bytes=16 << 20),
        cost_estimate=pl.CostEstimate(
            flops=2 * rows * features * vocab, bytes_accessed=6 << 20, transcendentals=0
        ),
        name="logits",
    )(h, head)


def target_column(ids_ref, at, offset):
    ids = ids_ref[at].astype(jnp.int32)
    lane = lax.broadcasted_iota(jnp.int32, ids.shape, 1)
    ids = jnp.where(lane == 0, ids * 4096, jnp.where(lane == 1, ids * 64, ids))
    return jnp.sum(ids.astype(F32), axis=1, keepdims=True).astype(jnp.int32) - offset


def own_kernel(offset_ref, ids_ref, x_ref, top_ref, power_ref, cols_ref):
    rows, vocab = x_ref.shape
    column = lax.broadcasted_iota(jnp.int32, (TILE, vocab), 1)

    @tiles(rows)
    def _(at):
        below = x_ref[at]
        top = top_ref[at, 0:1]
        power = jnp.exp(below)
        power_ref[at] = power
        hit = column == target_column(ids_ref, at, offset_ref[0])
        mine = jnp.sum(jnp.where(hit, below + top, 0.0), axis=1, keepdims=True)
        total = jnp.sum(power, axis=1, keepdims=True)
        cols_ref[at] = packed((top, total, None, mine), TILE)


def peer_half(x_ref, power_ref, cols_ref, got_ref, all_ref):
    rows = x_ref.shape[0]

    @tiles(rows)
    def _(at):
        below = -jnp.sqrt(jnp.sqrt(got_ref[at].astype(F32)))
        gap = x_ref[at] - below
        peer = jnp.exp(below)
        to_peer = jnp.sum(power_ref[at] * gap, axis=1, keepdims=True)
        total = jnp.sum(peer, axis=1, keepdims=True)
        to_own = -jnp.sum(peer * gap, axis=1, keepdims=True)
        all_ref[at] = cols_ref[at] + packed((None, None, to_peer, None, None, total, to_own), TILE)

    parts = []
    for b in range(rows // LANES):
        lanes = slice(b * LANES, (b + 1) * LANES)
        flat = jnp.transpose(all_ref[lanes])
        top, total = flat[0:1], flat[1:2]
        high, middle, low = (got_ref[rows : rows + 16, lanes].astype(F32)[i : i + 1] for i in range(3))
        peer_top = high + (middle + low)
        step = top - peer_top
        row = lax.broadcasted_iota(jnp.int32, (8, LANES), 0)
        out = flat[:8]
        out = jnp.where(row == 2, out + total * step, out)
        out = jnp.where(row == 4, peer_top, out)
        parts.append(jnp.where(row == 6, out - flat[5:6] * step, out))
    return jnp.concatenate(parts, axis=1)


def stats_near_kernel(x_ref, power_ref, cols_ref, got_ref, out_ref, all_ref):
    out_ref[...] = peer_half(x_ref, power_ref, cols_ref, got_ref, all_ref)


def stats_far_kernel(zh_ref, near_ref, x_ref, power_ref, cols_ref, got_ref, out_ref, all_ref):
    rows = x_ref.shape[0]
    far = peer_half(x_ref, power_ref, cols_ref, got_ref, all_ref)
    near_at = pl.ds(pl.multiple_of(zh_ref[0] * rows, rows), rows)
    far_at = pl.ds(pl.multiple_of((1 - zh_ref[0]) * rows, rows), rows)
    near = near_ref[...]
    for k in range(out_ref.shape[0]):
        out_ref[k, :, near_at] = near
        out_ref[k, :, far_at] = far


def merged(parts):
    out = []
    for first in (0, 4):
        top = jnp.max(parts[:, first], axis=0, keepdims=True)
        scale = jnp.exp(parts[:, first] - top)
        total = jnp.sum(parts[:, first + 1] * scale, axis=0, keepdims=True)
        mixed = jnp.sum(parts[:, first + 2] * scale, axis=0, keepdims=True)
        out += [top, total, mixed]
    return out[:3] + [jnp.sum(parts[:, 3], axis=0, keepdims=True)] + out[3:]


def merge_kernel(core_ref, in_ref, out_ref):
    count = out_ref.shape[2]
    values = merged(in_ref[:, :, pl.ds(pl.multiple_of(core_ref[0] * count, count), count)])
    values = jnp.concatenate(values + [jnp.zeros_like(values[0])], axis=0)
    for k in range(out_ref.shape[0]):
        out_ref[k] = values


def last_merge_kernel(in_ref, out_ref):
    values = merged(in_ref[...])
    out_ref[...] = jnp.concatenate(values + [jnp.zeros_like(values[0])], axis=0)


def grad_kernel(
    where_ref, whole_ref, local_ref, ids_ref, x_near, x_far, got_near, got_far,
    out_ref, loss_ref, flat_ref, cols_ref,
):
    step_at = pl.program_id(0)
    rows, vocab = out_ref.shape
    half = whole_ref.shape[2]

    @pl.when(step_at == 0)
    def _():
        flat_ref[...] = jnp.zeros_like(flat_ref)
        loss_ref[...] = jnp.zeros_like(loss_ref)
        for i in range(2):
            zh = where_ref[0] if i == 0 else 1 - where_ref[0]
            lanes = pl.ds(pl.multiple_of(zh * half, half), half)
            top, total, to_peer, target, peer_top, peer_total, to_own = (
                whole_ref[zh, k : k + 1, :] for k in range(7)
            )
            log_total = top + jnp.log(total)
            peer_log_total = peer_top + jnp.log(peer_total)
            step = log_total - peer_log_total
            reverse = to_peer / total - step
            forward_kl = to_own / peer_total + step
            loss_ref[0:1, lanes] = log_total - target + 0.5 * kl_weight * (forward_kl + reverse)
            own_top, own_peer_top = local_ref[0, 0:1, lanes], local_ref[0, 4:5, lanes]
            flat_ref[0:1] = jnp.exp(own_top - log_total)
            flat_ref[1:2] = (0.5 * kl_weight) * jnp.exp(own_peer_top - peer_log_total)
            flat_ref[2:3] = (1.0 + 0.5 * kl_weight) + 0.5 * kl_weight * (
                (own_top - own_peer_top) - step - reverse
            )
            for b in range(half // LANES):
                to = i * half + b * LANES
                cols_ref[to : to + LANES] = jnp.transpose(flat_ref[:, b * LANES : (b + 1) * LANES])

    def block(x_ref, got_ref):
        column = lax.broadcasted_iota(jnp.int32, (16, vocab), 1)

        @tiles(rows, 16)
        def _(at):
            here = pl.ds(pl.multiple_of(step_at * rows + at.start, 16), 16)
            below = x_ref[at]
            peer_below = -jnp.sqrt(jnp.sqrt(got_ref[at].astype(F32)))
            hit = column == target_column(ids_ref, at, where_ref[1])
            own_prob = jnp.exp(below) * cols_ref[here, 0:1]
            gap = below - peer_below
            inner = own_prob * (cols_ref[here, 2:3] + (0.5 * kl_weight) * gap)
            inner = inner - jnp.exp(peer_below) * cols_ref[here, 1:2] - jnp.where(hit, 1.0, 0.0)
            out_ref[at] = inner.astype(BF16)

    pl.when(step_at < 4)(lambda: block(x_near, got_near))
    pl.when(step_at >= 4)(lambda: block(x_far, got_far))


def logit_grads(where, whole, local, ids, x_near, x_far, got_near, got_far):
    half, vocab = x_near.shape
    rows = half // 4
    near = pl.BlockSpec((rows, vocab), lambda n, w: (jnp.minimum(n, 3), 0))
    far = pl.BlockSpec((rows, vocab), lambda n, w: (jnp.maximum(n - 4, 0), 0))

    def place(n, w):
        return (2 * (n % 4) + jnp.where(n < 4, w[0], 1 - w[0]), 0)

    return pl.pallas_call(
        grad_kernel,
        out_shape=[shape(2 * half, vocab, dtype=BF16), shape(8, 2 * half)],
        grid_spec=pltpu.PrefetchScalarGridSpec(
            num_scalar_prefetch=1,
            grid=(8,),
            in_specs=[
                pl.BlockSpec(whole.shape, lambda n, w: (0, 0, 0)),
                pl.BlockSpec(local.shape, lambda n, w: (0, 0, 0)),
                pl.BlockSpec((rows, LANES), lambda n, w: (n, 0)),
                near,
                far,
                near,
                far,
            ],
            out_specs=[
                pl.BlockSpec((rows, vocab), place),
                pl.BlockSpec((8, 2 * half), lambda n, w: (0, 0)),
            ],
            scratch_shapes=[pltpu.VMEM((LANES, half), F32), pltpu.VMEM((2 * half, LANES), F32)],
        ),
        compiler_params=pltpu.CompilerParams(vmem_limit_bytes=16 << 20),
        cost_estimate=pl.CostEstimate(flops=1, bytes_accessed=4 << 20, transcendentals=0),
        name="logit_grads",
    )(where, whole, local, ids, x_near, x_far, got_near, got_far)


def backward_kernel(half_ref, g_ref, w_ref, out_ref):
    depth = out_ref.shape[1]
    first = half_ref[0] * depth
    for n in range(0, depth, 256):
        width = min(256, depth - n)
        rows = w_ref[0, pl.ds(pl.multiple_of(first + n, LANES), width), :]
        out_ref[:, n : n + width] = lax.dot_general(
            g_ref[...], rows, (((1,), (1,)), ((), ())), preferred_element_type=F32
        ).astype(out_ref.dtype)


def backward(half, grads, head, dtype):
    rows, depth = grads.shape[0], head.shape[1] // 2
    return call(
        backward_kernel,
        [shape(rows, depth, dtype=dtype)],
        (half, grads, head),
        "head_grads",
        flops=2 * rows * depth * head.shape[2],
    )


def spread(block):
    out = lax.all_to_all(jnp.broadcast_to(block[None], (4,) + block.shape), "y", 0, 0)
    return out.reshape(-1, block.shape[1])


def logits_of(block, head):
    h = lax.all_gather(block[:, : head.shape[1] // 2], "c", axis=1, tiled=True)
    return forward(h, head)


def own_of(offset, ids, x, top):
    outs = [shape(*x.shape), shape(x.shape[0], LANES)]
    return call(own_kernel, outs, (offset, ids, x, top), "own_stats")


def exchange(partner, near, far, head, where):
    to_learner = [(partner[r], r) for r in range(4)]
    near_ids, x_near, sent, top_near = near
    offset = where[1:2]
    half = x_near.shape[0]
    depth = head.shape[1] // 2
    got_near = lax.ppermute(sent, "x", to_learner)
    far_h = spread(far)
    far_ids = far_h[:, depth:]
    x_far, sent, top_far = logits_of(far_h, head)
    sent, x_near = lax.optimization_barrier((sent, x_near))
    got_far = lax.ppermute(sent, "x", to_learner)
    power_near, cols_near = own_of(offset, near_ids, x_near, top_near)
    power_far, cols_far = own_of(offset, far_ids, x_far, top_far)
    scratch = [pltpu.VMEM((half, LANES), F32)]
    near = call(
        stats_near_kernel,
        [shape(8, half)],
        (x_near, power_near, cols_near, got_near),
        "near_stats",
        scratch,
    )
    local = call(
        stats_far_kernel,
        [shape(8, 8, 2 * half)],
        (where, near, x_far, power_far, cols_far, got_far),
        "far_stats",
        scratch,
    )
    return local, far_ids, x_far, got_near, got_far


def on_device(hidden, head_weight, targets, pairing, token_weight):
    zl, c, zh, y = (lax.axis_index(a) for a in ("zl", "c", "zh", "y"))
    rows, features = hidden.shape[1], hidden.shape[2]
    depth = features // 2
    vocab = head_weight.shape[2]
    offset = (((zl * 2 + c) * 2 + zh) * 4 + y) * vocab
    half = 4 * rows
    core = c.reshape(1)
    where = jnp.stack([zh, offset])

    ids = jnp.stack([targets >> 12, (targets >> 6) & 63, targets & 63], axis=1).astype(BF16)
    mine = jnp.concatenate(
        [
            lax.dynamic_slice_in_dim(hidden[0], c * depth, depth, 1),
            jnp.pad(ids, ((0, 0), (0, LANES - 3))),
        ],
        axis=1,
    )
    far = lax.ppermute(mine, ("zl", "zh"), SWAP_Z)
    near_h = spread(mine)
    near_ids = near_h[:, depth:]
    x_near, sent, top_near = logits_of(near_h, head_weight)
    x_near, far = lax.optimization_barrier((x_near, far))
    first, second = pairing[0], pairing[1]
    which = jnp.where(first == 2, jnp.where(second == 3, 0, 3), jnp.where(first == 3, 1, 2))
    local, far_ids, x_far, got_near, got_far = lax.switch(
        which,
        [functools.partial(exchange, p) for p in PAIRINGS],
        (near_ids, x_near, sent, top_near), far, head_weight, where,
    )

    parts = lax.all_to_all(local, ("c", "y"), 0, 0)
    parts = call(merge_kernel, [shape(16, 8, half)], (core, parts), "merge_near")
    parts = lax.all_to_all(parts, Z, 0, 0)
    parts = call(last_merge_kernel, [shape(8, half)], (parts,), "merge_all")
    whole = lax.all_gather(parts, "c", axis=0, tiled=False)
    ids = jnp.concatenate([near_ids, far_ids], axis=0)
    grads, losses = logit_grads(where, whole, local, ids, x_near, x_far, got_near, got_far)
    loss = lax.dynamic_slice(losses, (0, zh * half + y * rows), (1, rows))
    loss = token_weight * loss

    sent = lax.ppermute(backward(1 - core, grads, head_weight, BF16), "c", SWAP_C)
    kept = backward(core, grads, head_weight, F32)
    by_y = (kept + sent.astype(F32)).astype(BF16).reshape(4, 2 * rows, depth)
    by_y = lax.all_to_all(by_y, "y", 0, 0)
    by_z = jnp.sum(by_y.astype(F32), axis=0).astype(BF16).reshape(16, rows // 8, depth)
    by_z = lax.all_to_all(by_z, Z, 0, 0)
    weights = lax.dynamic_slice_in_dim(token_weight[0], zl * (rows // 8), rows // 8, 0)
    final = (jnp.sum(by_z.astype(F32), axis=0) * weights[:, None]).astype(BF16)
    final = lax.all_to_all(jnp.broadcast_to(final[None], (8,) + final.shape), "zl", 0, 0)
    final = lax.all_gather(final.reshape(rows, depth), "c", axis=1, tiled=True)
    return (final[None], loss)


def solution(mesh):
    fine = Mesh(mesh.devices.reshape(4, 8, 2, 2, 4), ("x", "zl", "c", "zh", "y"))
    return jax.shard_map(
        on_device,
        mesh=fine,
        in_specs=(
            P("x", ("zh", "y"), None),
            P("x", None, ("zl", "c", "zh", "y")),
            P(("zh", "y")),
            P(),
            P("x", ("zh", "y")),
        ),
        out_specs=(P("x", ("zh", "y"), None), P("x", ("zh", "y"))),
        check_vma=False,
    )
```

```python
import functools

import jax
import jax.numpy as jnp
from jax import lax
from jax.experimental import pallas as pl
from jax.experimental.pallas import tpu as pltpu
from jax.sharding import Mesh
from jax.sharding import PartitionSpec as P

kl_weight = 1.0
F32 = jnp.float32
BF16 = jnp.bfloat16
Z = ("zh", "zl")
FAR = {0: 12, 1: 13, 2: 14, 3: 15, 4: 8, 5: 9, 6: 10, 7: 11}
FAR.update({b: a for a, b in FAR.items()})
SWAP_Z = [(z % 8 * 2 + z // 8, FAR[z] % 8 * 2 + FAR[z] // 8) for z in range(16)]
SWAP_C = [(0, 1), (1, 0)]
PAIRINGS = ((2, 3, 1, 0), (3, 2, 0, 1), (1, 3, 0, 2), (2, 0, 3, 1))
LANES = 128
TILE = 32


def call(kernel, outs, operands, name, scratch=(), flops=0, stays=()):
    vmem, smem = pl.BlockSpec(memory_space=pltpu.VMEM), pl.BlockSpec(memory_space=pltpu.SMEM)
    specs = [smem if o.ndim == 1 else vmem for o in operands]
    for i in stays:
        specs[i] = pl.BlockSpec(memory_space=pl.ANY)
    moved = sum(o.size * o.dtype.itemsize for o in list(operands) + list(outs))
    return pl.pallas_call(
        kernel,
        out_shape=outs if len(outs) > 1 else outs[0],
        in_specs=specs,
        out_specs=[vmem] * len(outs) if len(outs) > 1 else vmem,
        scratch_shapes=scratch,
        compiler_params=pltpu.CompilerParams(vmem_limit_bytes=moved + (6 << 20)),
        cost_estimate=pl.CostEstimate(flops=flops, bytes_accessed=moved, transcendentals=0),
        name=name,
    )(*operands)


def shape(*dims, dtype=F32):
    return jax.ShapeDtypeStruct(dims, dtype)


def tiles(rows, step=TILE):
    def run(body):
        def at(i, carry):
            body(pl.ds(pl.multiple_of(i * step, step), step))
            return carry

        lax.fori_loop(0, rows // step, at, 0, unroll=True)

    return run


def packed(values, rows):
    lane = lax.broadcasted_iota(jnp.int32, (rows, LANES), 1)
    out = jnp.zeros((rows, LANES), F32)
    for i, v in enumerate(values):
        if v is not None:
            out = jnp.where(lane == i, v, out)
    return out


def hold_kernel(w_ref, out_ref, sem):
    copy = pltpu.make_async_copy(w_ref.at[0, : out_ref.shape[0]], out_ref, sem)
    copy.start()
    copy.wait()


def hold(head):
    return pl.pallas_call(
        hold_kernel,
        out_shape=jax.ShapeDtypeStruct((head.shape[1] // 2, head.shape[2]), head.dtype),
        in_specs=[pl.BlockSpec(memory_space=pl.ANY)],
        out_specs=pl.BlockSpec(memory_space=pltpu.VMEM),
        scratch_shapes=[pltpu.SemaphoreType.DMA(())],
        compiler_params=pltpu.CompilerParams(vmem_limit_bytes=8 << 20),
        cost_estimate=pl.CostEstimate(flops=0, bytes_accessed=4 << 20, transcendentals=0),
        name="hold_head",
    )(head)


def forward_kernel(h_ref, held_ref, w_ref, x_ref, sent_ref, top_ref, rest_ref, sem):
    depth = held_ref.shape[0]
    copy = pltpu.make_async_copy(w_ref.at[0, depth:], rest_ref, sem)
    copy.start()
    width = 512
    for n in range(0, x_ref.shape[1], width):
        at = slice(n, n + width)
        x_ref[:, at] = jnp.dot(h_ref[:, :depth], held_ref[:, at], preferred_element_type=F32)
    copy.wait()
    for n in range(0, x_ref.shape[1], width):
        at = slice(n, n + width)
        x_ref[:, at] += jnp.dot(h_ref[:, depth:], rest_ref[:, at], preferred_element_type=F32)
    below_top(x_ref, sent_ref, top_ref)


def below_top(x_ref, sent_ref, top_ref):
    rows, vocab = x_ref.shape

    @tiles(rows)
    def _(at):
        logits = x_ref[at]
        top = jnp.max(logits, axis=1, keepdims=True)
        below = logits - top
        x_ref[at] = below
        square = below * below
        sent_ref[at] = (square * square).astype(BF16)
        top_ref[at] = jnp.broadcast_to(top, (TILE, LANES))

    row = lax.broadcasted_iota(jnp.int32, (16, LANES), 0)
    sent_ref[rows:] = jnp.zeros((16, vocab), BF16)
    for b in range(rows // LANES):
        top = jnp.transpose(top_ref[b * LANES : (b + 1) * LANES])[:16]
        high = top.astype(BF16).astype(F32)
        middle = (top - high).astype(BF16).astype(F32)
        low = (top - high) - middle
        pieces = jnp.where(row == 0, high, jnp.where(row == 1, middle, low))
        pieces = jnp.where(row < 3, pieces, 0.0)
        sent_ref[rows:, b * LANES : (b + 1) * LANES] = pieces.astype(BF16)


def features_of(block):
    return lax.all_gather(block[:, : block.shape[1] - LANES], "c", axis=1, tiled=True)


def forward(h, held, head):
    rows, vocab = h.shape[0], head.shape[2]
    return call(
        forward_kernel,
        [shape(rows, vocab), shape(rows + 16, vocab, dtype=BF16), shape(rows, LANES)],
        (h, held, head),
        "logits",
        [pltpu.VMEM(held.shape, held.dtype), pltpu.SemaphoreType.DMA(())],
        flops=2 * rows * h.shape[1] * vocab,
        stays=(2,),
    )


def target_column(ids_ref, at, offset):
    ids = ids_ref[at, ids_ref.shape[1] - LANES :].astype(jnp.int32)
    lane = lax.broadcasted_iota(jnp.int32, ids.shape, 1)
    ids = jnp.where(lane == 0, ids * 4096, jnp.where(lane == 1, ids * 64, ids))
    return jnp.sum(ids.astype(F32), axis=1, keepdims=True).astype(jnp.int32) - offset


def own_kernel(offset_ref, ids_ref, x_ref, top_ref, power_ref, cols_ref):
    rows, vocab = x_ref.shape
    column = lax.broadcasted_iota(jnp.int32, (TILE, vocab), 1)

    @tiles(rows)
    def _(at):
        below = x_ref[at]
        top = top_ref[at, 0:1]
        power = jnp.exp(below)
        power_ref[at] = power
        hit = column == target_column(ids_ref, at, offset_ref[0])
        mine = jnp.sum(jnp.where(hit, below + top, 0.0), axis=1, keepdims=True)
        total = jnp.sum(power, axis=1, keepdims=True)
        cols_ref[at] = packed((top, total, None, mine), TILE)


def peer_half(x_ref, power_ref, cols_ref, got_ref, all_ref):
    rows = x_ref.shape[0]

    @tiles(rows)
    def _(at):
        below = -jnp.sqrt(jnp.sqrt(got_ref[at].astype(F32)))
        gap = x_ref[at] - below
        peer = jnp.exp(below)
        to_peer = jnp.sum(power_ref[at] * gap, axis=1, keepdims=True)
        total = jnp.sum(peer, axis=1, keepdims=True)
        to_own = -jnp.sum(peer * gap, axis=1, keepdims=True)
        all_ref[at] = cols_ref[at] + packed((None, None, to_peer, None, None, total, to_own), TILE)

    parts = []
    for b in range(rows // LANES):
        lanes = slice(b * LANES, (b + 1) * LANES)
        flat = jnp.transpose(all_ref[lanes])
        top, total = flat[0:1], flat[1:2]
        high, middle, low = (got_ref[rows : rows + 16, lanes].astype(F32)[i : i + 1] for i in range(3))
        peer_top = high + (middle + low)
        step = top - peer_top
        row = lax.broadcasted_iota(jnp.int32, (8, LANES), 0)
        out = flat[:8]
        out = jnp.where(row == 2, out + total * step, out)
        out = jnp.where(row == 4, peer_top, out)
        parts.append(jnp.where(row == 6, out - flat[5:6] * step, out))
    return jnp.concatenate(parts, axis=1)


def stats_near_kernel(x_ref, power_ref, cols_ref, got_ref, out_ref, all_ref):
    out_ref[...] = peer_half(x_ref, power_ref, cols_ref, got_ref, all_ref)


def stats_far_kernel(zh_ref, near_ref, x_ref, power_ref, cols_ref, got_ref, out_ref, all_ref):
    rows = x_ref.shape[0]
    far = peer_half(x_ref, power_ref, cols_ref, got_ref, all_ref)
    near_at = pl.ds(pl.multiple_of(zh_ref[0] * rows, rows), rows)
    far_at = pl.ds(pl.multiple_of((1 - zh_ref[0]) * rows, rows), rows)
    near = near_ref[...]
    for k in range(out_ref.shape[0]):
        out_ref[k, :, near_at] = near
        out_ref[k, :, far_at] = far


def merged(parts):
    out = []
    for first in (0, 4):
        top = jnp.max(parts[:, first], axis=0, keepdims=True)
        scale = jnp.exp(parts[:, first] - top)
        total = jnp.sum(parts[:, first + 1] * scale, axis=0, keepdims=True)
        mixed = jnp.sum(parts[:, first + 2] * scale, axis=0, keepdims=True)
        out += [top, total, mixed]
    return out[:3] + [jnp.sum(parts[:, 3], axis=0, keepdims=True)] + out[3:]


def merge_kernel(core_ref, in_ref, out_ref):
    count = out_ref.shape[2]
    values = merged(in_ref[:, :, pl.ds(pl.multiple_of(core_ref[0] * count, count), count)])
    values = jnp.concatenate(values + [jnp.zeros_like(values[0])], axis=0)
    for k in range(out_ref.shape[0]):
        out_ref[k] = values


def last_merge_kernel(in_ref, out_ref):
    values = merged(in_ref[...])
    out_ref[...] = jnp.concatenate(values + [jnp.zeros_like(values[0])], axis=0)


def grad_kernel(
    where_ref, whole_ref, local_ref, near_ids, far_ids, x_near, x_far, got_near, got_far,
    out_ref, loss_ref, flat_ref, cols_ref,
):
    half, vocab = x_near.shape
    quarter = half // 4
    flat_ref[...] = jnp.zeros_like(flat_ref)
    loss_ref[...] = jnp.zeros_like(loss_ref)
    column = lax.broadcasted_iota(jnp.int32, (TILE, vocab), 1)
    halves = (
        (where_ref[0], near_ids, x_near, got_near),
        (1 - where_ref[0], far_ids, x_far, got_far),
    )
    for zh, ids_ref, x_ref, got_ref in halves:
        lanes = pl.ds(pl.multiple_of(zh * half, half), half)
        top, total, to_peer, target, peer_top, peer_total, to_own = (
            whole_ref[zh, k : k + 1, :] for k in range(7)
        )
        log_total = top + jnp.log(total)
        peer_log_total = peer_top + jnp.log(peer_total)
        step = log_total - peer_log_total
        reverse = to_peer / total - step
        forward_kl = to_own / peer_total + step
        loss_ref[0:1, lanes] = log_total - target + 0.5 * kl_weight * (forward_kl + reverse)
        own_top, own_peer_top = local_ref[0, 0:1, lanes], local_ref[0, 4:5, lanes]
        flat_ref[0:1] = jnp.exp(own_top - log_total)
        flat_ref[1:2] = (0.5 * kl_weight) * jnp.exp(own_peer_top - peer_log_total)
        flat_ref[2:3] = (1.0 + 0.5 * kl_weight) + 0.5 * kl_weight * (
            (own_top - own_peer_top) - step - reverse
        )
        for b in range(half // LANES):
            block = slice(b * LANES, (b + 1) * LANES)
            cols_ref[block] = jnp.transpose(flat_ref[:, block])
        for i in range(half // TILE):
            at = slice(i * TILE, (i + 1) * TILE)
            y, t = divmod(i * TILE, quarter)
            below = x_ref[at]
            peer_below = -jnp.sqrt(jnp.sqrt(got_ref[at].astype(F32)))
            hit = column == target_column(ids_ref, at, where_ref[1])
            own_prob = jnp.exp(below) * cols_ref[at, 0:1]
            gap = below - peer_below
            inner = own_prob * (cols_ref[at, 2:3] + (0.5 * kl_weight) * gap)
            inner = inner - jnp.exp(peer_below) * cols_ref[at, 1:2] - jnp.where(hit, 1.0, 0.0)
            to = pl.multiple_of(2 * quarter * y + t + zh * quarter, TILE)
            out_ref[pl.ds(to, TILE)] = inner.astype(BF16)


def backward_kernel(half_ref, g_ref, w_ref, out_ref):
    depth = out_ref.shape[1]
    first = half_ref[0] * depth
    for n in range(0, depth, 256):
        width = min(256, depth - n)
        rows = w_ref[0, pl.ds(pl.multiple_of(first + n, LANES), width), :]
        out_ref[:, n : n + width] = lax.dot_general(
            g_ref[...], rows, (((1,), (1,)), ((), ())), preferred_element_type=F32
        ).astype(out_ref.dtype)


def backward(half, grads, head, dtype):
    rows, depth = grads.shape[0], head.shape[1] // 2
    return call(
        backward_kernel,
        [shape(rows, depth, dtype=dtype)],
        (half, grads, head),
        "head_grads",
        flops=2 * rows * depth * head.shape[2],
    )


def sum_kernel(in_ref, out_ref):
    total = in_ref[0].astype(F32)
    for k in range(1, in_ref.shape[0]):
        total = total + in_ref[k].astype(F32)
    out_ref[...] = total.astype(BF16)


def last_sum_kernel(in_ref, weight_ref, out_ref):
    total = in_ref[0].astype(F32)
    for k in range(1, in_ref.shape[0]):
        total = total + in_ref[k].astype(F32)
    total = (total * weight_ref[:, 0:1]).astype(BF16)
    for k in range(out_ref.shape[0]):
        out_ref[k] = total


def spread(block):
    out = lax.all_to_all(jnp.broadcast_to(block[None], (4,) + block.shape), "y", 0, 0)
    return out.reshape(-1, block.shape[1])


def own_of(offset, ids, x, top):
    outs = [shape(*x.shape), shape(x.shape[0], LANES)]
    return call(own_kernel, outs, (offset, ids, x, top), "own_stats")


def exchange(partner, near, far, head, where):
    to_learner = [(partner[r], r) for r in range(4)]
    near, x_near, sent, top_near = near
    offset = where[1:2]
    half = near.shape[0]
    got_near = lax.ppermute(sent, "x", to_learner)
    far = spread(far)
    x_far, sent, top_far = forward(features_of(far), hold(head), head)
    sent, x_near = lax.optimization_barrier((sent, x_near))
    got_far = lax.ppermute(sent, "x", to_learner)
    power_near, cols_near = own_of(offset, near, x_near, top_near)
    power_far, cols_far = own_of(offset, far, x_far, top_far)
    scratch = [pltpu.VMEM((half, LANES), F32)]
    near_stats = call(
        stats_near_kernel,
        [shape(8, half)],
        (x_near, power_near, cols_near, got_near),
        "near_stats",
        scratch,
    )
    local = call(
        stats_far_kernel,
        [shape(8, 8, 2 * half)],
        (where, near_stats, x_far, power_far, cols_far, got_far),
        "far_stats",
        scratch,
    )
    return local, far, x_near, x_far, got_near, got_far


def on_device(hidden, head_weight, targets, pairing, token_weight):
    zl, c, zh, y = (lax.axis_index(a) for a in ("zl", "c", "zh", "y"))
    rows, features = hidden.shape[1], hidden.shape[2]
    depth = features // 2
    vocab = head_weight.shape[2]
    offset = (((zl * 2 + c) * 2 + zh) * 4 + y) * vocab
    half = 4 * rows
    core = c.reshape(1)
    where = jnp.stack([zh, offset])

    ids = jnp.stack([targets >> 12, (targets >> 6) & 63, targets & 63], axis=1).astype(BF16)
    mine = jnp.concatenate(
        [
            lax.dynamic_slice_in_dim(hidden[0], c * depth, depth, 1),
            jnp.pad(ids, ((0, 0), (0, LANES - 3))),
        ],
        axis=1,
    )
    far = lax.ppermute(mine, ("zl", "zh"), SWAP_Z)
    near = spread(mine)
    x_near, sent, top_near = forward(features_of(near), hold(head_weight), head_weight)
    x_near, far = lax.optimization_barrier((x_near, far))
    first, second = pairing[0], pairing[1]
    which = jnp.where(first == 2, jnp.where(second == 3, 0, 3), jnp.where(first == 3, 1, 2))
    local, far, x_near, x_far, got_near, got_far = lax.switch(
        which,
        [functools.partial(exchange, p) for p in PAIRINGS],
        (near, x_near, sent, top_near), far, head_weight, where,
    )

    parts = lax.all_to_all(local, ("c", "y"), 0, 0)
    parts = call(merge_kernel, [shape(16, 8, half)], (core, parts), "merge_near")
    parts = lax.all_to_all(parts, Z, 0, 0)
    parts = call(last_merge_kernel, [shape(8, half)], (parts,), "merge_all")
    whole = lax.all_gather(parts, "c", axis=0, tiled=False)
    grads, losses = call(
        grad_kernel,
        [shape(2 * half, vocab, dtype=BF16), shape(8, 2 * half)],
        (where, whole, local, near, far, x_near, x_far, got_near, got_far),
        "logit_grads",
        [pltpu.VMEM((LANES, half), F32), pltpu.VMEM((half, LANES), F32)],
    )
    loss = lax.dynamic_slice(losses, (0, zh * half + y * rows), (1, rows))
    loss = token_weight * loss

    sent = lax.ppermute(backward(1 - core, grads, head_weight, BF16), "c", SWAP_C)
    kept = backward(core, grads, head_weight, F32)
    by_y = (kept + sent.astype(F32)).astype(BF16).reshape(4, 2 * rows, depth)
    by_y = lax.all_to_all(by_y, "y", 0, 0)
    by_z = call(sum_kernel, [shape(2 * rows, depth, dtype=BF16)], (by_y,), "sum_y")
    by_z = lax.all_to_all(by_z.reshape(16, rows // 8, depth), Z, 0, 0)
    weights = lax.dynamic_slice_in_dim(token_weight[0], zl * (rows // 8), rows // 8, 0)
    final = call(
        last_sum_kernel,
        [shape(8, rows // 8, depth, dtype=BF16)],
        (by_z, jnp.broadcast_to(weights[:, None], (rows // 8, LANES))),
        "sum_z",
    )
    final = lax.all_to_all(final, "zl", 0, 0)
    final = lax.all_gather(final.reshape(rows, depth), "c", axis=1, tiled=True)
    return (final[None], loss)


def solution(mesh):
    fine = Mesh(mesh.devices.reshape(4, 8, 2, 2, 4), ("x", "zl", "c", "zh", "y"))
    return jax.shard_map(
        on_device,
        mesh=fine,
        in_specs=(
            P("x", ("zh", "y"), None),
            P("x", None, ("zl", "c", "zh", "y")),
            P(("zh", "y")),
            P(),
            P("x", ("zh", "y")),
        ),
        out_specs=(P("x", ("zh", "y"), None), P("x", ("zh", "y"))),
        check_vma=False,
    )
```

```python
import functools

import jax
import jax.numpy as jnp
from jax import lax
from jax.experimental import pallas as pl
from jax.experimental.pallas import tpu as pltpu
from jax.sharding import Mesh
from jax.sharding import PartitionSpec as P

kl_weight = 1.0
F32 = jnp.float32
BF16 = jnp.bfloat16
Z = ("zh", "zl")
FAR = {0: 12, 1: 13, 2: 14, 3: 15, 4: 8, 5: 9, 6: 10, 7: 11}
FAR.update({b: a for a, b in FAR.items()})
SWAP_Z = [(z % 8 * 2 + z // 8, FAR[z] % 8 * 2 + FAR[z] // 8) for z in range(16)]
SWAP_C = [(0, 1), (1, 0)]
PAIRINGS = ((2, 3, 1, 0), (3, 2, 0, 1), (1, 3, 0, 2), (2, 0, 3, 1))
LANES = 128
TILE = 32


def call(kernel, outs, operands, name, scratch=(), flops=0, stays=()):
    vmem, smem = pl.BlockSpec(memory_space=pltpu.VMEM), pl.BlockSpec(memory_space=pltpu.SMEM)
    specs = [smem if o.ndim == 1 else vmem for o in operands]
    for i in stays:
        specs[i] = pl.BlockSpec(memory_space=pl.ANY)
    moved = sum(o.size * o.dtype.itemsize for o in list(operands) + list(outs))
    return pl.pallas_call(
        kernel,
        out_shape=outs if len(outs) > 1 else outs[0],
        in_specs=specs,
        out_specs=[vmem] * len(outs) if len(outs) > 1 else vmem,
        scratch_shapes=scratch,
        compiler_params=pltpu.CompilerParams(vmem_limit_bytes=moved + (6 << 20)),
        cost_estimate=pl.CostEstimate(flops=flops, bytes_accessed=moved, transcendentals=0),
        name=name,
    )(*operands)


def shape(*dims, dtype=F32):
    return jax.ShapeDtypeStruct(dims, dtype)


def tiles(rows, step=TILE):
    def run(body):
        def at(i, carry):
            body(pl.ds(pl.multiple_of(i * step, step), step))
            return carry

        lax.fori_loop(0, rows // step, at, 0, unroll=True)

    return run


def packed(values, rows):
    lane = lax.broadcasted_iota(jnp.int32, (rows, LANES), 1)
    out = jnp.zeros((rows, LANES), F32)
    for i, v in enumerate(values):
        if v is not None:
            out = jnp.where(lane == i, v, out)
    return out


def hold_kernel(w_ref, out_ref, sem):
    copy = pltpu.make_async_copy(w_ref.at[0, : out_ref.shape[0]], out_ref, sem)
    copy.start()
    copy.wait()


def hold(head):
    return pl.pallas_call(
        hold_kernel,
        out_shape=jax.ShapeDtypeStruct((head.shape[1] // 2, head.shape[2]), head.dtype),
        in_specs=[pl.BlockSpec(memory_space=pl.ANY)],
        out_specs=pl.BlockSpec(memory_space=pltpu.VMEM),
        scratch_shapes=[pltpu.SemaphoreType.DMA(())],
        compiler_params=pltpu.CompilerParams(vmem_limit_bytes=8 << 20),
        cost_estimate=pl.CostEstimate(flops=0, bytes_accessed=4 << 20, transcendentals=0),
        name="hold_head",
    )(head)


def forward_kernel(h_ref, held_ref, w_ref, x_ref, sent_ref, top_ref, rest_ref, sem):
    depth = held_ref.shape[0]
    copy = pltpu.make_async_copy(w_ref.at[0, depth:], rest_ref, sem)
    copy.start()
    width = 512
    for n in range(0, x_ref.shape[1], width):
        at = slice(n, n + width)
        x_ref[:, at] = jnp.dot(h_ref[:, :depth], held_ref[:, at], preferred_element_type=F32)
    copy.wait()
    for n in range(0, x_ref.shape[1], width):
        at = slice(n, n + width)
        x_ref[:, at] += jnp.dot(h_ref[:, depth:], rest_ref[:, at], preferred_element_type=F32)
    below_top(x_ref, sent_ref, top_ref)


def below_top(x_ref, sent_ref, top_ref):
    rows, vocab = x_ref.shape

    @tiles(rows)
    def _(at):
        logits = x_ref[at]
        top = jnp.max(logits, axis=1, keepdims=True)
        below = logits - top
        x_ref[at] = below
        square = below * below
        sent_ref[at] = (square * square).astype(BF16)
        top_ref[at] = jnp.broadcast_to(top, (TILE, LANES))

    row = lax.broadcasted_iota(jnp.int32, (16, LANES), 0)
    sent_ref[rows:] = jnp.zeros((16, vocab), BF16)
    for b in range(rows // LANES):
        top = jnp.transpose(top_ref[b * LANES : (b + 1) * LANES])[:16]
        high = top.astype(BF16).astype(F32)
        middle = (top - high).astype(BF16).astype(F32)
        low = (top - high) - middle
        pieces = jnp.where(row == 0, high, jnp.where(row == 1, middle, low))
        pieces = jnp.where(row < 3, pieces, 0.0)
        sent_ref[rows:, b * LANES : (b + 1) * LANES] = pieces.astype(BF16)


def features_of(block):
    return lax.all_gather(block[:, : block.shape[1] - LANES], "c", axis=1, tiled=True)


def forward(h, held, head):
    rows, vocab = h.shape[0], head.shape[2]
    return call(
        forward_kernel,
        [shape(rows, vocab), shape(rows + 16, vocab, dtype=BF16), shape(rows, LANES)],
        (h, held, head),
        "logits",
        [pltpu.VMEM(held.shape, held.dtype), pltpu.SemaphoreType.DMA(())],
        flops=2 * rows * h.shape[1] * vocab,
        stays=(2,),
    )


def target_column(ids_ref, at, offset):
    ids = ids_ref[at, ids_ref.shape[1] - LANES :].astype(jnp.int32)
    lane = lax.broadcasted_iota(jnp.int32, ids.shape, 1)
    ids = jnp.where(lane == 0, ids * 4096, jnp.where(lane == 1, ids * 64, ids))
    return jnp.sum(ids.astype(F32), axis=1, keepdims=True).astype(jnp.int32) - offset


def own_kernel(offset_ref, ids_ref, x_ref, top_ref, power_ref, cols_ref):
    rows, vocab = x_ref.shape
    column = lax.broadcasted_iota(jnp.int32, (TILE, vocab), 1)

    @tiles(rows)
    def _(at):
        below = x_ref[at]
        top = top_ref[at, 0:1]
        power = jnp.exp(below)
        power_ref[at] = power
        hit = column == target_column(ids_ref, at, offset_ref[0])
        mine = jnp.sum(jnp.where(hit, below + top, 0.0), axis=1, keepdims=True)
        total = jnp.sum(power, axis=1, keepdims=True)
        cols_ref[at] = packed((top, total, None, mine), TILE)


def decoded(sent):
    return -lax.rsqrt(lax.rsqrt(jnp.maximum(sent.astype(F32), 1e-37)))


def peer_half(x_ref, power_ref, cols_ref, got_ref, all_ref):
    rows = x_ref.shape[0]

    @tiles(rows)
    def _(at):
        below = decoded(got_ref[at])
        gap = x_ref[at] - below
        peer = jnp.exp(below)
        to_peer = jnp.sum(power_ref[at] * gap, axis=1, keepdims=True)
        total = jnp.sum(peer, axis=1, keepdims=True)
        to_own = -jnp.sum(peer * gap, axis=1, keepdims=True)
        all_ref[at] = cols_ref[at] + packed((None, None, to_peer, None, None, total, to_own), TILE)

    parts = []
    for b in range(rows // LANES):
        lanes = slice(b * LANES, (b + 1) * LANES)
        flat = jnp.transpose(all_ref[lanes])
        top, total = flat[0:1], flat[1:2]
        high, middle, low = (got_ref[rows : rows + 16, lanes].astype(F32)[i : i + 1] for i in range(3))
        peer_top = high + (middle + low)
        step = top - peer_top
        row = lax.broadcasted_iota(jnp.int32, (8, LANES), 0)
        out = flat[:8]
        out = jnp.where(row == 2, out + total * step, out)
        out = jnp.where(row == 4, peer_top, out)
        parts.append(jnp.where(row == 6, out - flat[5:6] * step, out))
    return jnp.concatenate(parts, axis=1)


def stats_near_kernel(x_ref, power_ref, cols_ref, got_ref, out_ref, all_ref):
    out_ref[...] = peer_half(x_ref, power_ref, cols_ref, got_ref, all_ref)


def stats_far_kernel(zh_ref, near_ref, x_ref, power_ref, cols_ref, got_ref, out_ref, all_ref):
    rows = x_ref.shape[0]
    far = peer_half(x_ref, power_ref, cols_ref, got_ref, all_ref)
    near_at = pl.ds(pl.multiple_of(zh_ref[0] * rows, rows), rows)
    far_at = pl.ds(pl.multiple_of((1 - zh_ref[0]) * rows, rows), rows)
    near = near_ref[...]
    for k in range(out_ref.shape[0]):
        out_ref[k, :, near_at] = near
        out_ref[k, :, far_at] = far


def merged(parts):
    out = []
    for first in (0, 4):
        top = jnp.max(parts[:, first], axis=0, keepdims=True)
        scale = jnp.exp(parts[:, first] - top)
        total = jnp.sum(parts[:, first + 1] * scale, axis=0, keepdims=True)
        mixed = jnp.sum(parts[:, first + 2] * scale, axis=0, keepdims=True)
        out += [top, total, mixed]
    return out[:3] + [jnp.sum(parts[:, 3], axis=0, keepdims=True)] + out[3:]


def merge_kernel(core_ref, in_ref, out_ref):
    count = out_ref.shape[2]
    values = merged(in_ref[:, :, pl.ds(pl.multiple_of(core_ref[0] * count, count), count)])
    values = jnp.concatenate(values + [jnp.zeros_like(values[0])], axis=0)
    for k in range(out_ref.shape[0]):
        out_ref[k] = values


def last_merge_kernel(in_ref, out_ref):
    values = merged(in_ref[...])
    out_ref[...] = jnp.concatenate(values + [jnp.zeros_like(values[0])], axis=0)


def grad_kernel(
    where_ref, whole_ref, local_ref, near_ids, far_ids, x_near, x_far, got_near, got_far,
    out_ref, loss_ref, flat_ref, cols_ref,
):
    half, vocab = x_near.shape
    quarter = half // 4
    flat_ref[...] = jnp.zeros_like(flat_ref)
    loss_ref[...] = jnp.zeros_like(loss_ref)
    column = lax.broadcasted_iota(jnp.int32, (TILE, vocab), 1)
    halves = (
        (where_ref[0], near_ids, x_near, got_near),
        (1 - where_ref[0], far_ids, x_far, got_far),
    )
    for zh, ids_ref, x_ref, got_ref in halves:
        lanes = pl.ds(pl.multiple_of(zh * half, half), half)
        top, total, to_peer, target, peer_top, peer_total, to_own = (
            whole_ref[zh, k : k + 1, :] for k in range(7)
        )
        log_total = top + jnp.log(total)
        peer_log_total = peer_top + jnp.log(peer_total)
        step = log_total - peer_log_total
        reverse = to_peer / total - step
        forward_kl = to_own / peer_total + step
        loss_ref[0:1, lanes] = log_total - target + 0.5 * kl_weight * (forward_kl + reverse)
        own_top, own_peer_top = local_ref[0, 0:1, lanes], local_ref[0, 4:5, lanes]
        flat_ref[0:1] = jnp.exp(own_top - log_total)
        flat_ref[1:2] = (0.5 * kl_weight) * jnp.exp(own_peer_top - peer_log_total)
        flat_ref[2:3] = (1.0 + 0.5 * kl_weight) + 0.5 * kl_weight * (
            (own_top - own_peer_top) - step - reverse
        )
        for b in range(half // LANES):
            block = slice(b * LANES, (b + 1) * LANES)
            cols_ref[block] = jnp.transpose(flat_ref[:, block])
        for i in range(half // TILE):
            at = slice(i * TILE, (i + 1) * TILE)
            y, t = divmod(i * TILE, quarter)
            below = x_ref[at]
            peer_below = decoded(got_ref[at])
            hit = column == target_column(ids_ref, at, where_ref[1])
            own_prob = jnp.exp(below) * cols_ref[at, 0:1]
            gap = below - peer_below
            inner = own_prob * (cols_ref[at, 2:3] + (0.5 * kl_weight) * gap)
            inner = inner - jnp.exp(peer_below) * cols_ref[at, 1:2] - jnp.where(hit, 1.0, 0.0)
            to = pl.multiple_of(2 * quarter * y + t + zh * quarter, TILE)
            out_ref[pl.ds(to, TILE)] = inner.astype(BF16)


def backward_kernel(half_ref, g_ref, w_ref, out_ref):
    depth = out_ref.shape[1]
    first = half_ref[0] * depth
    for n in range(0, depth, 256):
        width = min(256, depth - n)
        rows = w_ref[0, pl.ds(pl.multiple_of(first + n, LANES), width), :]
        out_ref[:, n : n + width] = lax.dot_general(
            g_ref[...], rows, (((1,), (1,)), ((), ())), preferred_element_type=F32
        ).astype(out_ref.dtype)


def backward(half, grads, head, dtype):
    rows, depth = grads.shape[0], head.shape[1] // 2
    return call(
        backward_kernel,
        [shape(rows, depth, dtype=dtype)],
        (half, grads, head),
        "head_grads",
        flops=2 * rows * depth * head.shape[2],
    )


def sum_kernel(in_ref, out_ref):
    total = in_ref[0].astype(F32)
    for k in range(1, in_ref.shape[0]):
        total = total + in_ref[k].astype(F32)
    out_ref[...] = total.astype(BF16)


def last_sum_kernel(in_ref, weight_ref, out_ref):
    total = in_ref[0].astype(F32)
    for k in range(1, in_ref.shape[0]):
        total = total + in_ref[k].astype(F32)
    total = (total * weight_ref[:, 0:1]).astype(BF16)
    for k in range(out_ref.shape[0]):
        out_ref[k] = total


def spread(block):
    out = lax.all_to_all(jnp.broadcast_to(block[None], (4,) + block.shape), "y", 0, 0)
    return out.reshape(-1, block.shape[1])


def own_of(offset, ids, x, top):
    outs = [shape(*x.shape), shape(x.shape[0], LANES)]
    return call(own_kernel, outs, (offset, ids, x, top), "own_stats")


def exchange(partner, near, far, head, where):
    to_learner = [(partner[r], r) for r in range(4)]
    near, x_near, sent, top_near = near
    offset = where[1:2]
    half = near.shape[0]
    got_near = lax.ppermute(sent, "x", to_learner)
    far = spread(far)
    x_far, sent, top_far = forward(features_of(far), hold(head), head)
    sent, x_near = lax.optimization_barrier((sent, x_near))
    got_far = lax.ppermute(sent, "x", to_learner)
    power_near, cols_near = own_of(offset, near, x_near, top_near)
    power_far, cols_far = own_of(offset, far, x_far, top_far)
    scratch = [pltpu.VMEM((half, LANES), F32)]
    near_stats = call(
        stats_near_kernel,
        [shape(8, half)],
        (x_near, power_near, cols_near, got_near),
        "near_stats",
        scratch,
    )
    local = call(
        stats_far_kernel,
        [shape(8, 8, 2 * half)],
        (where, near_stats, x_far, power_far, cols_far, got_far),
        "far_stats",
        scratch,
    )
    return local, far, x_near, x_far, got_near, got_far


def on_device(hidden, head_weight, targets, pairing, token_weight):
    zl, c, zh, y = (lax.axis_index(a) for a in ("zl", "c", "zh", "y"))
    rows, features = hidden.shape[1], hidden.shape[2]
    depth = features // 2
    vocab = head_weight.shape[2]
    offset = (((zl * 2 + c) * 2 + zh) * 4 + y) * vocab
    half = 4 * rows
    core = c.reshape(1)
    where = jnp.stack([zh, offset])

    ids = jnp.stack([targets >> 12, (targets >> 6) & 63, targets & 63], axis=1).astype(BF16)
    mine = jnp.concatenate(
        [
            lax.dynamic_slice_in_dim(hidden[0], c * depth, depth, 1),
            jnp.pad(ids, ((0, 0), (0, LANES - 3))),
        ],
        axis=1,
    )
    far = lax.ppermute(mine, ("zl", "zh"), SWAP_Z)
    near = spread(mine)
    x_near, sent, top_near = forward(features_of(near), hold(head_weight), head_weight)
    x_near, far = lax.optimization_barrier((x_near, far))
    first, second = pairing[0], pairing[1]
    which = jnp.where(first == 2, jnp.where(second == 3, 0, 3), jnp.where(first == 3, 1, 2))
    local, far, x_near, x_far, got_near, got_far = lax.switch(
        which,
        [functools.partial(exchange, p) for p in PAIRINGS],
        (near, x_near, sent, top_near), far, head_weight, where,
    )

    parts = lax.all_to_all(local, ("c", "y"), 0, 0)
    parts = call(merge_kernel, [shape(16, 8, half)], (core, parts), "merge_near")
    parts = lax.all_to_all(parts, Z, 0, 0)
    parts = call(last_merge_kernel, [shape(8, half)], (parts,), "merge_all")
    whole = lax.all_gather(parts, "c", axis=0, tiled=False)
    grads, losses = call(
        grad_kernel,
        [shape(2 * half, vocab, dtype=BF16), shape(8, 2 * half)],
        (where, whole, local, near, far, x_near, x_far, got_near, got_far),
        "logit_grads",
        [pltpu.VMEM((LANES, half), F32), pltpu.VMEM((half, LANES), F32)],
    )
    loss = lax.dynamic_slice(losses, (0, zh * half + y * rows), (1, rows))
    loss = token_weight * loss

    sent = lax.ppermute(backward(1 - core, grads, head_weight, BF16), "c", SWAP_C)
    kept = backward(core, grads, head_weight, F32)
    by_y = (kept + sent.astype(F32)).astype(BF16).reshape(4, 2 * rows, depth)
    by_y = lax.all_to_all(by_y, "y", 0, 0)
    by_z = call(sum_kernel, [shape(2 * rows, depth, dtype=BF16)], (by_y,), "sum_y")
    by_z = lax.all_to_all(by_z.reshape(16, rows // 8, depth), Z, 0, 0)
    weights = lax.dynamic_slice_in_dim(token_weight[0], zl * (rows // 8), rows // 8, 0)
    final = call(
        last_sum_kernel,
        [shape(8, rows // 8, depth, dtype=BF16)],
        (by_z, jnp.broadcast_to(weights[:, None], (rows // 8, LANES))),
        "sum_z",
    )
    final = lax.all_to_all(final, "zl", 0, 0)
    final = lax.all_gather(final.reshape(rows, depth), "c", axis=1, tiled=True)
    return (final[None], loss)


def solution(mesh):
    fine = Mesh(mesh.devices.reshape(4, 8, 2, 2, 4), ("x", "zl", "c", "zh", "y"))
    return jax.shard_map(
        on_device,
        mesh=fine,
        in_specs=(
            P("x", ("zh", "y"), None),
            P("x", None, ("zl", "c", "zh", "y")),
            P(("zh", "y")),
            P(),
            P("x", ("zh", "y")),
        ),
        out_specs=(P("x", ("zh", "y"), None), P("x", ("zh", "y"))),
        check_vma=False,
    )
```

```python
import functools

import jax
import jax.numpy as jnp
from jax import lax
from jax.experimental import pallas as pl
from jax.experimental.pallas import tpu as pltpu
from jax.sharding import Mesh
from jax.sharding import PartitionSpec as P

kl_weight = 1.0
F32 = jnp.float32
BF16 = jnp.bfloat16
Z = ("zh", "zl")
FAR = {0: 12, 1: 13, 2: 14, 3: 15, 4: 8, 5: 9, 6: 10, 7: 11}
FAR.update({b: a for a, b in FAR.items()})
SWAP_Z = [(z % 8 * 2 + z // 8, FAR[z] % 8 * 2 + FAR[z] // 8) for z in range(16)]
SWAP_C = [(0, 1), (1, 0)]
PAIRINGS = ((2, 3, 1, 0), (3, 2, 0, 1), (1, 3, 0, 2), (2, 0, 3, 1))
LANES = 128
TILE = 32


def call(kernel, outs, operands, name, scratch=(), flops=0, stays=()):
    vmem, smem = pl.BlockSpec(memory_space=pltpu.VMEM), pl.BlockSpec(memory_space=pltpu.SMEM)
    specs = [smem if o.ndim == 1 else vmem for o in operands]
    for i in stays:
        specs[i] = pl.BlockSpec(memory_space=pl.ANY)
    moved = sum(o.size * o.dtype.itemsize for o in list(operands) + list(outs))
    return pl.pallas_call(
        kernel,
        out_shape=outs if len(outs) > 1 else outs[0],
        in_specs=specs,
        out_specs=[vmem] * len(outs) if len(outs) > 1 else vmem,
        scratch_shapes=scratch,
        compiler_params=pltpu.CompilerParams(vmem_limit_bytes=moved + (6 << 20)),
        cost_estimate=pl.CostEstimate(flops=flops, bytes_accessed=moved, transcendentals=0),
        name=name,
    )(*operands)


def shape(*dims, dtype=F32):
    return jax.ShapeDtypeStruct(dims, dtype)


def tiles(rows, step=TILE):
    def run(body):
        def at(i, carry):
            body(pl.ds(pl.multiple_of(i * step, step), step))
            return carry

        lax.fori_loop(0, rows // step, at, 0, unroll=True)

    return run


def packed(values, rows):
    lane = lax.broadcasted_iota(jnp.int32, (rows, LANES), 1)
    out = jnp.zeros((rows, LANES), F32)
    for i, v in enumerate(values):
        if v is not None:
            out = jnp.where(lane == i, v, out)
    return out


def hold_kernel(w_ref, out_ref, sem):
    copy = pltpu.make_async_copy(w_ref.at[0, : out_ref.shape[0]], out_ref, sem)
    copy.start()
    copy.wait()


def hold(head):
    return pl.pallas_call(
        hold_kernel,
        out_shape=jax.ShapeDtypeStruct((head.shape[1] // 2, head.shape[2]), head.dtype),
        in_specs=[pl.BlockSpec(memory_space=pl.ANY)],
        out_specs=pl.BlockSpec(memory_space=pltpu.VMEM),
        scratch_shapes=[pltpu.SemaphoreType.DMA(())],
        compiler_params=pltpu.CompilerParams(vmem_limit_bytes=8 << 20),
        cost_estimate=pl.CostEstimate(flops=0, bytes_accessed=4 << 20, transcendentals=0),
        name="hold_head",
    )(head)


def forward_kernel(h_ref, held_ref, w_ref, x_ref, first_ref, second_ref, top_ref, rest_ref, sem):
    depth = held_ref.shape[0]
    copy = pltpu.make_async_copy(w_ref.at[0, depth:], rest_ref, sem)
    copy.start()
    width = 512
    for n in range(0, x_ref.shape[1], width):
        at = slice(n, n + width)
        x_ref[:, at] = jnp.dot(h_ref[:, :depth], held_ref[:, at], preferred_element_type=F32)
    copy.wait()
    for n in range(0, x_ref.shape[1], width):
        at = slice(n, n + width)
        x_ref[:, at] += jnp.dot(h_ref[:, depth:], rest_ref[:, at], preferred_element_type=F32)
    below_top(x_ref, first_ref, second_ref, top_ref)


def rows_of(first_ref, second_ref, i):
    count = first_ref.shape[0] // TILE
    ref = first_ref if i < count else second_ref
    return ref, slice(i % count * TILE, (i % count + 1) * TILE)


def below_top(x_ref, first_ref, second_ref, top_ref):
    rows, vocab = x_ref.shape

    for i in range(rows // TILE):
        at = slice(i * TILE, (i + 1) * TILE)
        part_ref, part_at = rows_of(first_ref, second_ref, i)
        logits = x_ref[at]
        top = jnp.max(logits, axis=1, keepdims=True)
        below = logits - top
        x_ref[at] = below
        square = below * below
        part_ref[part_at] = (square * square).astype(BF16)
        top_ref[at] = jnp.broadcast_to(top, (TILE, LANES))

    row = lax.broadcasted_iota(jnp.int32, (16, LANES), 0)
    end = rows // 2
    second_ref[end:] = jnp.zeros((16, vocab), BF16)
    for b in range(rows // LANES):
        top = jnp.transpose(top_ref[b * LANES : (b + 1) * LANES])[:16]
        high = top.astype(BF16).astype(F32)
        middle = (top - high).astype(BF16).astype(F32)
        low = (top - high) - middle
        pieces = jnp.where(row == 0, high, jnp.where(row == 1, middle, low))
        pieces = jnp.where(row < 3, pieces, 0.0)
        second_ref[end:, b * LANES : (b + 1) * LANES] = pieces.astype(BF16)


def features_of(block):
    return lax.all_gather(block[:, : block.shape[1] - LANES], "c", axis=1, tiled=True)


def forward(h, held, head):
    rows, vocab = h.shape[0], head.shape[2]
    return call(
        forward_kernel,
        [
            shape(rows, vocab),
            shape(rows // 2, vocab, dtype=BF16),
            shape(rows // 2 + 16, vocab, dtype=BF16),
            shape(rows, LANES),
        ],
        (h, held, head),
        "logits",
        [pltpu.VMEM(held.shape, held.dtype), pltpu.SemaphoreType.DMA(())],
        flops=2 * rows * h.shape[1] * vocab,
        stays=(2,),
    )


def target_column(ids_ref, at, offset):
    ids = ids_ref[at, ids_ref.shape[1] - LANES :].astype(jnp.int32)
    lane = lax.broadcasted_iota(jnp.int32, ids.shape, 1)
    ids = jnp.where(lane == 0, ids * 4096, jnp.where(lane == 1, ids * 64, ids))
    return jnp.sum(ids.astype(F32), axis=1, keepdims=True).astype(jnp.int32) - offset


def own_kernel(offset_ref, ids_ref, x_ref, top_ref, power_ref, cols_ref):
    rows, vocab = x_ref.shape
    column = lax.broadcasted_iota(jnp.int32, (TILE, vocab), 1)

    @tiles(rows)
    def _(at):
        below = x_ref[at]
        top = top_ref[at, 0:1]
        power = jnp.exp(below)
        power_ref[at] = power
        hit = column == target_column(ids_ref, at, offset_ref[0])
        mine = jnp.sum(jnp.where(hit, below + top, 0.0), axis=1, keepdims=True)
        total = jnp.sum(power, axis=1, keepdims=True)
        cols_ref[at] = packed((top, total, None, mine), TILE)


def decoded(sent):
    return -lax.rsqrt(lax.rsqrt(jnp.maximum(sent.astype(F32), 1e-37)))


def peer_half(x_ref, power_ref, cols_ref, first_ref, second_ref, all_ref):
    rows = x_ref.shape[0]
    end = rows // 2

    for i in range(rows // TILE):
        at = slice(i * TILE, (i + 1) * TILE)
        part_ref, part_at = rows_of(first_ref, second_ref, i)
        below = decoded(part_ref[part_at])
        gap = x_ref[at] - below
        peer = jnp.exp(below)
        to_peer = jnp.sum(power_ref[at] * gap, axis=1, keepdims=True)
        total = jnp.sum(peer, axis=1, keepdims=True)
        to_own = -jnp.sum(peer * gap, axis=1, keepdims=True)
        all_ref[at] = cols_ref[at] + packed((None, None, to_peer, None, None, total, to_own), TILE)

    parts = []
    for b in range(rows // LANES):
        lanes = slice(b * LANES, (b + 1) * LANES)
        flat = jnp.transpose(all_ref[lanes])
        top, total = flat[0:1], flat[1:2]
        high, middle, low = (second_ref[end : end + 16, lanes].astype(F32)[i : i + 1] for i in range(3))
        peer_top = high + (middle + low)
        step = top - peer_top
        row = lax.broadcasted_iota(jnp.int32, (8, LANES), 0)
        out = flat[:8]
        out = jnp.where(row == 2, out + total * step, out)
        out = jnp.where(row == 4, peer_top, out)
        parts.append(jnp.where(row == 6, out - flat[5:6] * step, out))
    return jnp.concatenate(parts, axis=1)


def stats_near_kernel(x_ref, power_ref, cols_ref, first_ref, second_ref, out_ref, all_ref):
    out_ref[...] = peer_half(x_ref, power_ref, cols_ref, first_ref, second_ref, all_ref)


def stats_far_kernel(
    zh_ref, near_ref, x_ref, power_ref, cols_ref, first_ref, second_ref, out_ref, all_ref
):
    rows = x_ref.shape[0]
    far = peer_half(x_ref, power_ref, cols_ref, first_ref, second_ref, all_ref)
    near_at = pl.ds(pl.multiple_of(zh_ref[0] * rows, rows), rows)
    far_at = pl.ds(pl.multiple_of((1 - zh_ref[0]) * rows, rows), rows)
    near = near_ref[...]
    for k in range(out_ref.shape[0]):
        out_ref[k, :, near_at] = near
        out_ref[k, :, far_at] = far


def merged(parts):
    out = []
    for first in (0, 4):
        top = jnp.max(parts[:, first], axis=0, keepdims=True)
        scale = jnp.exp(parts[:, first] - top)
        total = jnp.sum(parts[:, first + 1] * scale, axis=0, keepdims=True)
        mixed = jnp.sum(parts[:, first + 2] * scale, axis=0, keepdims=True)
        out += [top, total, mixed]
    return out[:3] + [jnp.sum(parts[:, 3], axis=0, keepdims=True)] + out[3:]


def merge_kernel(core_ref, in_ref, out_ref):
    count = out_ref.shape[2]
    values = merged(in_ref[:, :, pl.ds(pl.multiple_of(core_ref[0] * count, count), count)])
    values = jnp.concatenate(values + [jnp.zeros_like(values[0])], axis=0)
    for k in range(out_ref.shape[0]):
        out_ref[k] = values


def last_merge_kernel(in_ref, out_ref):
    values = merged(in_ref[...])
    out_ref[...] = jnp.concatenate(values + [jnp.zeros_like(values[0])], axis=0)


def grad_kernel(
    where_ref, whole_ref, local_ref, near_ids, far_ids, x_near, x_far,
    near_first, near_second, far_first, far_second, out_ref, loss_ref, flat_ref, cols_ref,
):
    half, vocab = x_near.shape
    quarter = half // 4
    flat_ref[...] = jnp.zeros_like(flat_ref)
    loss_ref[...] = jnp.zeros_like(loss_ref)
    column = lax.broadcasted_iota(jnp.int32, (TILE, vocab), 1)
    halves = (
        (where_ref[0], near_ids, x_near, (near_first, near_second)),
        (1 - where_ref[0], far_ids, x_far, (far_first, far_second)),
    )
    for zh, ids_ref, x_ref, got_refs in halves:
        lanes = pl.ds(pl.multiple_of(zh * half, half), half)
        top, total, to_peer, target, peer_top, peer_total, to_own = (
            whole_ref[zh, k : k + 1, :] for k in range(7)
        )
        log_total = top + jnp.log(total)
        peer_log_total = peer_top + jnp.log(peer_total)
        step = log_total - peer_log_total
        reverse = to_peer / total - step
        forward_kl = to_own / peer_total + step
        loss_ref[0:1, lanes] = log_total - target + 0.5 * kl_weight * (forward_kl + reverse)
        own_top, own_peer_top = local_ref[0, 0:1, lanes], local_ref[0, 4:5, lanes]
        flat_ref[0:1] = jnp.exp(own_top - log_total)
        flat_ref[1:2] = (0.5 * kl_weight) * jnp.exp(own_peer_top - peer_log_total)
        flat_ref[2:3] = (1.0 + 0.5 * kl_weight) + 0.5 * kl_weight * (
            (own_top - own_peer_top) - step - reverse
        )
        for b in range(half // LANES):
            block = slice(b * LANES, (b + 1) * LANES)
            cols_ref[block] = jnp.transpose(flat_ref[:, block])
        for i in range(half // TILE):
            at = slice(i * TILE, (i + 1) * TILE)
            y, t = divmod(i * TILE, quarter)
            below = x_ref[at]
            part_ref, part_at = rows_of(*got_refs, i)
            peer_below = decoded(part_ref[part_at])
            hit = column == target_column(ids_ref, at, where_ref[1])
            own_prob = jnp.exp(below) * cols_ref[at, 0:1]
            gap = below - peer_below
            inner = own_prob * (cols_ref[at, 2:3] + (0.5 * kl_weight) * gap)
            inner = inner - jnp.exp(peer_below) * cols_ref[at, 1:2] - jnp.where(hit, 1.0, 0.0)
            to = pl.multiple_of(2 * quarter * y + t + zh * quarter, TILE)
            out_ref[pl.ds(to, TILE)] = inner.astype(BF16)


def backward_kernel(half_ref, g_ref, w_ref, out_ref):
    depth = out_ref.shape[1]
    first = half_ref[0] * depth
    for n in range(0, depth, 256):
        width = min(256, depth - n)
        rows = w_ref[0, pl.ds(pl.multiple_of(first + n, LANES), width), :]
        out_ref[:, n : n + width] = lax.dot_general(
            g_ref[...], rows, (((1,), (1,)), ((), ())), preferred_element_type=F32
        ).astype(out_ref.dtype)


def backward(half, grads, head, dtype):
    rows, depth = grads.shape[0], head.shape[1] // 2
    return call(
        backward_kernel,
        [shape(rows, depth, dtype=dtype)],
        (half, grads, head),
        "head_grads",
        flops=2 * rows * depth * head.shape[2],
    )


def sum_kernel(in_ref, out_ref):
    total = in_ref[0].astype(F32)
    for k in range(1, in_ref.shape[0]):
        total = total + in_ref[k].astype(F32)
    out_ref[...] = total.astype(BF16)


def last_sum_kernel(in_ref, weight_ref, out_ref):
    total = in_ref[0].astype(F32)
    for k in range(1, in_ref.shape[0]):
        total = total + in_ref[k].astype(F32)
    total = (total * weight_ref[:, 0:1]).astype(BF16)
    for k in range(out_ref.shape[0]):
        out_ref[k] = total


def spread(block):
    out = lax.all_to_all(jnp.broadcast_to(block[None], (4,) + block.shape), "y", 0, 0)
    return out.reshape(-1, block.shape[1])


def own_of(offset, ids, x, top):
    outs = [shape(*x.shape), shape(x.shape[0], LANES)]
    return call(own_kernel, outs, (offset, ids, x, top), "own_stats")


def exchange(partner, near, far, head, where):
    to_learner = [(partner[r], r) for r in range(4)]
    near, x_near, sent, top_near = near
    offset = where[1:2]
    half = near.shape[0]
    got_near = [lax.ppermute(p, "x", to_learner) for p in sent]
    far = spread(far)
    x_far, *sent, top_far = forward(features_of(far), hold(head), head)
    sent, x_near = lax.optimization_barrier((sent, x_near))
    got_far = [lax.ppermute(p, "x", to_learner) for p in sent]
    power_near, cols_near = own_of(offset, near, x_near, top_near)
    power_far, cols_far = own_of(offset, far, x_far, top_far)
    scratch = [pltpu.VMEM((half, LANES), F32)]
    near_stats = call(
        stats_near_kernel,
        [shape(8, half)],
        (x_near, power_near, cols_near, *got_near),
        "near_stats",
        scratch,
    )
    local = call(
        stats_far_kernel,
        [shape(8, 8, 2 * half)],
        (where, near_stats, x_far, power_far, cols_far, *got_far),
        "far_stats",
        scratch,
    )
    return local, far, x_near, x_far, got_near, got_far


def on_device(hidden, head_weight, targets, pairing, token_weight):
    zl, c, zh, y = (lax.axis_index(a) for a in ("zl", "c", "zh", "y"))
    rows, features = hidden.shape[1], hidden.shape[2]
    depth = features // 2
    vocab = head_weight.shape[2]
    offset = (((zl * 2 + c) * 2 + zh) * 4 + y) * vocab
    half = 4 * rows
    core = c.reshape(1)
    where = jnp.stack([zh, offset])

    ids = jnp.stack([targets >> 12, (targets >> 6) & 63, targets & 63], axis=1).astype(BF16)
    mine = jnp.concatenate(
        [
            lax.dynamic_slice_in_dim(hidden[0], c * depth, depth, 1),
            jnp.pad(ids, ((0, 0), (0, LANES - 3))),
        ],
        axis=1,
    )
    far = lax.ppermute(mine, ("zl", "zh"), SWAP_Z)
    near = spread(mine)
    x_near, *sent, top_near = forward(features_of(near), hold(head_weight), head_weight)
    x_near, far = lax.optimization_barrier((x_near, far))
    first, second = pairing[0], pairing[1]
    which = jnp.where(first == 2, jnp.where(second == 3, 0, 3), jnp.where(first == 3, 1, 2))
    local, far, x_near, x_far, got_near, got_far = lax.switch(
        which,
        [functools.partial(exchange, p) for p in PAIRINGS],
        (near, x_near, sent, top_near), far, head_weight, where,
    )

    parts = lax.all_to_all(local, ("c", "y"), 0, 0)
    parts = call(merge_kernel, [shape(16, 8, half)], (core, parts), "merge_near")
    parts = lax.all_to_all(parts, Z, 0, 0)
    parts = call(last_merge_kernel, [shape(8, half)], (parts,), "merge_all")
    whole = lax.all_gather(parts, "c", axis=0, tiled=False)
    grads, losses = call(
        grad_kernel,
        [shape(2 * half, vocab, dtype=BF16), shape(8, 2 * half)],
        (where, whole, local, near, far, x_near, x_far, *got_near, *got_far),
        "logit_grads",
        [pltpu.VMEM((LANES, half), F32), pltpu.VMEM((half, LANES), F32)],
    )
    loss = lax.dynamic_slice(losses, (0, zh * half + y * rows), (1, rows))
    loss = token_weight * loss

    sent = lax.ppermute(backward(1 - core, grads, head_weight, BF16), "c", SWAP_C)
    kept = backward(core, grads, head_weight, F32)
    by_y = (kept + sent.astype(F32)).astype(BF16).reshape(4, 2 * rows, depth)
    by_y = lax.all_to_all(by_y, "y", 0, 0)
    by_z = call(sum_kernel, [shape(2 * rows, depth, dtype=BF16)], (by_y,), "sum_y")
    by_z = lax.all_to_all(by_z.reshape(16, rows // 8, depth), Z, 0, 0)
    weights = lax.dynamic_slice_in_dim(token_weight[0], zl * (rows // 8), rows // 8, 0)
    final = call(
        last_sum_kernel,
        [shape(8, rows // 8, depth, dtype=BF16)],
        (by_z, jnp.broadcast_to(weights[:, None], (rows // 8, LANES))),
        "sum_z",
    )
    final = lax.all_to_all(final, "zl", 0, 0)
    final = lax.all_gather(final.reshape(rows, depth), "c", axis=1, tiled=True)
    return (final[None], loss)


def solution(mesh):
    fine = Mesh(mesh.devices.reshape(4, 8, 2, 2, 4), ("x", "zl", "c", "zh", "y"))
    return jax.shard_map(
        on_device,
        mesh=fine,
        in_specs=(
            P("x", ("zh", "y"), None),
            P("x", None, ("zl", "c", "zh", "y")),
            P(("zh", "y")),
            P(),
            P("x", ("zh", "y")),
        ),
        out_specs=(P("x", ("zh", "y"), None), P("x", ("zh", "y"))),
        check_vma=False,
    )
```
